32 devices in a mesh: cross: 16 (over z, y, core), height: 2 (over x).
Axes of the slice: x: 2, y: 2, z: 4, core: 2. Of those that a mesh axis runs over, the one named last changes fastest.
Arguments:
- state: float32 [4, 16, 256, 512], P(None, 'height', 'cross'), may hold values from -6 to 6
- turbulence: bfloat16 [2, 16, 256, 512], P(None, 'height', 'cross'), may hold values from -2 to 2
- wind: float32 [16], P('height'), may hold values from 0.05 to 0.35
- ground_admittance: float32 [256, 512], P('cross'), may hold values from 0.2 to 2
- ground_kind: int32 [256, 512], P('cross'), may hold values 0 or 1
- drift_cells: int32 [2, 16], P(None, 'height'), may hold values from 0 to 255
- drift_eighths: int32 [2, 16], P(None, 'height'), may hold values from 0 to 7
Outputs:
- state_out: float32 [4, 16, 256, 512], P(None, 'height', 'cross')
The draws below stay inside these ranges and needn't reach their ends.
All inputs are finite; a program needn't handle non-finite values. No bound on the sum of `ground_kind` on one device may be relied on, other than what follows from the above.
Results may differ from the reference program's by a relative error of at most 0.0015.
Values may be sent and summed in bfloat16 or wider, within the bound.
A program may use at most 64 MiB of HBM per device.

```python
import math
import jax
import jax.numpy as jnp

RANGE = 512
STEPS = 2
NY = 256
NZ = 16


def set_ends(result, stream_key, least, high):
    longest = result.shape.index(max(result.shape))
    spots = []
    for shift in (0, 1):
        where = [jax.random.randint(jax.random.fold_in(stream_key, axis), (), 0, length) for axis, length in enumerate(result.shape)]
        where[longest] = (where[longest] + shift) % result.shape[longest]
        spots.append(tuple(where))
    return result.at[spots[0]].set(least).at[spots[1]].set(high)


def block_levels(rng, dims, split, smallest, largest):
    gain = 1.0
    for axis_at, shards_of in split:
        draws = jax.random.uniform(jax.random.fold_in(jax.random.fold_in(rng, 6), axis_at), (shards_of,), jnp.float32, smallest / len(split), largest / len(split))
        gain = gain * jnp.repeat(jnp.exp(draws), dims[axis_at] // shards_of).reshape((-1,) + (1,) * (len(dims) - 1 - axis_at))
    return gain


def noise(stream_key, shape, width, reach, cuts=(), kind=jnp.bfloat16):
    entries = jax.random.normal(stream_key, shape, jnp.float32) * width
    if len(cuts) > 0:
        entries = block_levels(stream_key, shape, cuts, -0.22, 0.18) * entries
    return jnp.clip(entries, min=-reach, max=reach).astype(kind)


def setup_inputs(seed: int = 0) -> dict:
    key_list = jax.random.split(jax.random.key(seed), 8)
    state = noise(key_list[0], (4, NZ, NY, RANGE), 1.0, 6.0, ((1, 2), (2, 16)), jnp.float32)
    turbulence = noise(key_list[1], (2, NZ, NY, RANGE), 0.15, 2.0, ((1, 2), (2, 16)))
    wind = jnp.clip(0.05 + 0.29999999 * jax.random.uniform(key_list[2], (NZ,), jnp.float32) ** block_levels(key_list[2], (NZ,), ((0, 2),), -0.2, 0.2), 0.05, 0.35)
    ground_admittance = jnp.clip(jnp.exp(math.log(2.0) - 2.3025851 * jax.random.uniform(key_list[3], (NY, RANGE), jnp.float32) ** block_levels(key_list[3], (NY, RANGE), ((0, 16),), -0.2, 0.2)), 0.2, 2.0)
    ground_kind = set_ends((jax.random.randint(key_list[4], (NY, RANGE), 0, 2) < 1).astype(jnp.int32), jax.random.fold_in(key_list[4], 1), 0, 1)
    drift_cells = set_ends(jax.random.randint(key_list[5], (STEPS, NZ), 0, NY), jax.random.fold_in(key_list[5], 1), 0, NY - 1).astype(jnp.int32)
    drift_eighths = set_ends(jax.random.randint(key_list[6], (STEPS, NZ), 0, 8), jax.random.fold_in(key_list[6], 1), 0, 7).astype(jnp.int32)
    return dict(state=state, turbulence=turbulence, wind=wind, ground_admittance=ground_admittance, ground_kind=ground_kind, drift_cells=drift_cells, drift_eighths=drift_eighths)


section_keep = (0.0, -5.0 / 9.0, -153.0 / 128.0)
section_gain = (1.0 / 3.0, 15.0 / 16.0, 8.0 / 15.0)
time_step = 0.4


def place_level(level, cells, eighths):
    moved = jnp.roll(level, cells, axis=1)
    first = moved.astype(jnp.float32)
    second = jnp.roll(moved, 1, axis=1).astype(jnp.float32)
    weight = eighths.astype(jnp.float32) / 8.0
    return (1.0 - weight) * first + weight * second


def along_range(field):
    padded = jnp.pad(field, [(0, 0)] * (field.ndim - 1) + [(1, 1)])
    return 0.5 * (padded[..., 2:] - padded[..., :-2])


def rates(state, advect, squared, ground):
    pressure, vel_cross, vel_up = state[0], state[2], state[3]
    cross_p = jnp.pad(pressure, ((0, 0), (1, 1), (0, 0)))
    cross_v = jnp.pad(vel_cross, ((0, 0), (1, 1), (0, 0)))
    low_p = pressure[0]
    low_w = ground * pressure[0] - vel_up[0]
    top_zero = jnp.zeros_like(pressure[:1])
    upper_p = jnp.concatenate([low_p[None], pressure, top_zero], axis=0)
    upper_w = jnp.concatenate([low_w[None], vel_up, top_zero], axis=0)
    dy_p = 0.5 * (cross_p[:, 2:] - cross_p[:, :-2])
    dy_v = 0.5 * (cross_v[:, 2:] - cross_v[:, :-2])
    dz_p = 0.5 * (upper_p[2:] - upper_p[:-2])
    dz_w = 0.5 * (upper_w[2:] - upper_w[:-2])
    slope = along_range(state)
    rate_p = -advect * slope[0] - squared * (slope[1] + dy_v + dz_w)
    rate_u = -advect * slope[1] - slope[0]
    rate_v = -advect * slope[2] - dy_p
    rate_w = -advect * slope[3] - dz_p
    return jnp.stack([rate_p, rate_u, rate_v, rate_w])


def reference(state, turbulence, wind, ground_admittance, ground_kind, drift_cells, drift_eighths):
    ground = 2.0 * ground_admittance * ground_kind.astype(jnp.float32)
    current = state
    for step in range(STEPS):
        frozen = jax.vmap(place_level, in_axes=(1, 0, 0), out_axes=1)(
            turbulence, drift_cells[step].astype(jnp.int32), drift_eighths[step])
        advect = wind[:, None, None] + frozen[0]
        squared = (1.0 + frozen[1]) * (1.0 + frozen[1])
        change = jnp.zeros_like(current)
        for section in range(3):
            change = section_keep[section] * change + time_step * rates(current, advect, squared, ground)
            current = current + section_gain[section] * change
    return current
```

```python
import functools
import math

import jax
import jax.numpy as jnp
from jax import lax
from jax.experimental import pallas as pl
from jax.experimental.pallas import tpu as pltpu
from jax.sharding import PartitionSpec as P

section_keep = (0.0, -5.0 / 9.0, -153.0 / 128.0)
section_gain = (1.0 / 3.0, 15.0 / 16.0, 8.0 / 15.0)
time_step = 0.4
half_step = 0.5 * time_step
MESH = pl.DeviceIdType.MESH


def kernel(
    n, floors, steps, levels, rows, cols, width,
    state_ref, turb_ref, wind_ref, adm_ref, kind_ref, cells_ref, eighths_ref,
    out_ref,
    pa, ua, va, wa, pb, ub, vb, wb, chg, adv, sqr, gath, outb, froz,
    rsend, rrecv, hsend, hrecv,
    in_sem, s1, r1, s2, r2, rs, rr, hs, hr,
):
    me = lax.axis_index("cross")
    floor = lax.axis_index("height")
    length = n * rows
    pieces = cols // width
    sections = 3 * steps

    def part(j):
        field = j // (levels * pieces)
        rest = j % (levels * pieces)
        return field, rest // pieces, pl.multiple_of((rest % pieces) * width, width)

    def peer(k):
        return lax.rem(me + k, n)

    def rows_of(j):
        return pl.ds(pl.multiple_of(j * rows, rows), rows)

    has_left, has_right = me > 0, me < n - 1
    has_below, has_above = floor > 0, floor < floors - 1

    loads = [
        pltpu.make_async_copy(state_ref.at[0], pa.at[pl.ds(1, levels)], in_sem.at[0]),
        pltpu.make_async_copy(state_ref.at[1], ua, in_sem.at[1]),
        pltpu.make_async_copy(state_ref.at[2], va, in_sem.at[2]),
        pltpu.make_async_copy(state_ref.at[3], wa.at[pl.ds(1, levels)], in_sem.at[3]),
    ]
    for load in loads:
        load.start()

    barrier = pltpu.get_barrier_semaphore()

    def greet(k, carry):
        pl.semaphore_signal(barrier, inc=1, device_id={"cross": peer(k)}, device_id_type=MESH)
        return carry

    lax.fori_loop(1, n, greet, 0)

    @pl.when(has_below)
    def _():
        pl.semaphore_signal(barrier, inc=1, device_id={"height": floor - 1}, device_id_type=MESH)

    @pl.when(has_above)
    def _():
        pl.semaphore_signal(barrier, inc=1, device_id={"height": floor + 1}, device_id_type=MESH)

    zero_rows = jnp.zeros((2 * levels, cols), jnp.float32)
    for k in range(sections):
        @pl.when(jnp.logical_not(has_left))
        def _():
            rrecv[k, 0] = zero_rows

        @pl.when(jnp.logical_not(has_right))
        def _():
            rrecv[k, 1] = zero_rows

    pl.semaphore_wait(
        barrier, n - 1 + has_below.astype(jnp.int32) + has_above.astype(jnp.int32)
    )

    def gather_copy(k):
        to = peer(k)
        field, level, at = part(to)
        return pltpu.make_async_remote_copy(
            src_ref=turb_ref.at[field, level, :, pl.ds(at, width)],
            dst_ref=gath.at[rows_of(me)],
            send_sem=s1.at[to],
            recv_sem=r1.at[me],
            device_id={"cross": to},
            device_id_type=MESH,
        )

    def gather_wait(k):
        source = peer(k)
        return pltpu.make_async_remote_copy(
            src_ref=gath.at[rows_of(source)],
            dst_ref=gath.at[rows_of(source)],
            send_sem=s1.at[source],
            recv_sem=r1.at[source],
            device_id={"cross": source},
            device_id_type=MESH,
        )

    def start_gather(k, carry):
        gather_copy(k).start()
        return carry

    lax.fori_loop(1, n, start_gather, 0)
    my_field, my_level, my_at = part(me)
    own = pltpu.make_async_copy(
        turb_ref.at[my_field, my_level, :, pl.ds(my_at, width)], gath.at[rows_of(me)], in_sem.at[4]
    )
    own.start()

    def row_copy(k, side):
        to = me - 1 if side == 0 else me + 1
        return pltpu.make_async_remote_copy(
            src_ref=rsend.at[k, side],
            dst_ref=rrecv.at[k, 1 - side],
            send_sem=rs.at[k, side],
            recv_sem=rr.at[k, 1 - side],
            device_id={"cross": to},
            device_id_type=MESH,
        )

    def level_copy(k, side):
        to = floor - 1 if side == 0 else floor + 1
        return pltpu.make_async_remote_copy(
            src_ref=hsend.at[k, side],
            dst_ref=hrecv.at[k, 1 - side],
            send_sem=hs.at[k, side],
            recv_sem=hr.at[k, 1 - side],
            device_id={"height": to},
            device_id_type=MESH,
        )

    def send_rows(k):
        @pl.when(has_left)
        def _():
            row_copy(k, 0).start()

        @pl.when(has_right)
        def _():
            row_copy(k, 1).start()

    def send_levels(k, pn, wn):
        @pl.when(has_below)
        def _():
            hsend[k, 0, 0] = pn[1].astype(jnp.bfloat16)
            hsend[k, 0, 1] = wn[1].astype(jnp.bfloat16)
            level_copy(k, 0).start()

        @pl.when(has_above)
        def _():
            hsend[k, 1, 0] = pn[levels].astype(jnp.bfloat16)
            hsend[k, 1, 1] = wn[levels].astype(jnp.bfloat16)
            level_copy(k, 1).start()

    def receive(k, pn, wn):
        @pl.when(has_below)
        def _():
            level_copy(k, 1).wait_recv()
            pn[0] = hrecv[k, 0, 0].astype(jnp.float32)
            wn[0] = hrecv[k, 0, 1].astype(jnp.float32)

        @pl.when(jnp.logical_not(has_below))
        def _():
            ground = 2.0 * adm_ref[...] * kind_ref[...].astype(jnp.float32)
            low = pn[1]
            pn[0] = low
            wn[0] = ground * low - wn[1]

        @pl.when(has_above)
        def _():
            level_copy(k, 0).wait_recv()
            pn[levels + 1] = hrecv[k, 1, 0].astype(jnp.float32)
            wn[levels + 1] = hrecv[k, 1, 1].astype(jnp.float32)

        @pl.when(jnp.logical_not(has_above))
        def _():
            pn[levels + 1] = jnp.zeros((rows, cols), jnp.float32)
            wn[levels + 1] = jnp.zeros((rows, cols), jnp.float32)

        @pl.when(has_left)
        def _():
            row_copy(k, 1).wait_recv()

        @pl.when(has_right)
        def _():
            row_copy(k, 0).wait_recv()

    for load in loads:
        load.wait()

    def first_rows(level, carry):
        for field, ref, offset in ((0, pa, 1), (1, va, 0)):
            rsend[0, 0, pl.ds(field * levels + level, 1)] = ref[level + offset, pl.ds(0, 1)]
            rsend[0, 1, pl.ds(field * levels + level, 1)] = ref[level + offset, pl.ds(rows - 1, 1)]
        return carry

    lax.fori_loop(0, levels, first_rows, 0)
    send_rows(0)
    send_levels(0, pa, wa)

    own.wait()

    def whole(k, carry):
        gather_wait(k).wait_recv()
        return carry

    lax.fori_loop(1, n, whole, 0)
    block = math.gcd(length, 256)

    def spread_copy(step, k):
        to = peer(k)
        return pltpu.make_async_remote_copy(
            src_ref=outb.at[step, rows_of(to)],
            dst_ref=froz.at[step, my_field, my_level, :, pl.ds(my_at, width)],
            send_sem=s2.at[step, to],
            recv_sem=r2.at[step, me],
            device_id={"cross": to},
            device_id_type=MESH,
        )

    def spread_wait(step, k):
        source = peer(k)
        field, level, at = part(source)
        return pltpu.make_async_remote_copy(
            src_ref=outb.at[step, rows_of(source)],
            dst_ref=froz.at[step, field, level, :, pl.ds(at, width)],
            send_sem=s2.at[step, source],
            recv_sem=r2.at[step, source],
            device_id={"cross": source},
            device_id_type=MESH,
        )

    for step in range(steps):
        cells = cells_ref[step, my_level]
        weight = eighths_ref[step, my_level].astype(jnp.float32) / 8.0

        def mix(i, carry, step=step, cells=cells, weight=weight):
            top = pl.multiple_of(i * block, block)
            to_row = lax.broadcasted_iota(jnp.int32, (block, length), 0) + top
            from_row = lax.broadcasted_iota(jnp.int32, (block, length), 1)
            back = to_row - from_row - cells
            back = jnp.where(back < 0, back + length, back)
            back = jnp.where(back < 0, back + length, back)
            share = jnp.where(back == 0, 1.0 - weight, jnp.where(back == 1, weight, 0.0))
            outb[step, pl.ds(top, block)] = jnp.dot(
                share.astype(jnp.bfloat16), gath[...], preferred_element_type=jnp.float32
            ).astype(jnp.bfloat16)
            return carry

        lax.fori_loop(0, length // block, mix, 0)

        def spread(k, carry, step=step):
            spread_copy(step, k).start()
            return carry

        lax.fori_loop(1, n, spread, 0)
        froz[step, my_field, my_level, :, pl.ds(my_at, width)] = outb[step, rows_of(me)]

    row_id = lax.broadcasted_iota(jnp.int32, (rows, cols), 0)
    col_id = lax.broadcasted_iota(jnp.int32, (rows, cols), 1)

    def d_range(f):
        ahead = jnp.where(col_id == cols - 1, 0.0, pltpu.roll(f, cols - 1, 1))
        behind = jnp.where(col_id == 0, 0.0, pltpu.roll(f, 1, 1))
        return ahead - behind

    def d_cross(f, before, after):
        ahead = jnp.where(row_id == rows - 1, after, pltpu.roll(f, rows - 1, 0))
        behind = jnp.where(row_id == 0, before, pltpu.roll(f, 1, 0))
        return ahead - behind

    sets = ((pa, ua, va, wa), (pb, ub, vb, wb))
    for k in range(sections):
        step, section = k // 3, k % 3
        po, uo, vo, wo = sets[k % 2]
        pn, un, vn, wn = sets[(k + 1) % 2]
        last = k == sections - 1
        if section == 0:
            def arrive(j, carry, step=step):
                spread_wait(step, j).wait_recv()
                return carry

            lax.fori_loop(1, n, arrive, 0)
        receive(k, po, wo)
        keep, gain = section_keep[section], section_gain[section]

        def update(level, carry):
            if section == 0:
                frozen = froz[step, 0, level].astype(jnp.float32)
                speed = 1.0 + froz[step, 1, level].astype(jnp.float32)
                advect = half_step * (wind_ref[level] + frozen)
                squared = half_step * (speed * speed)
                adv[level] = advect
                sqr[level] = squared
            else:
                advect = adv[level]
                squared = sqr[level]
            p, u, v, w = po[level + 1], uo[level], vo[level], wo[level + 1]
            p_x, u_x, v_x, w_x = d_range(p), d_range(u), d_range(v), d_range(w)
            p_y = d_cross(p, rrecv[k, 0, pl.ds(level, 1)], rrecv[k, 1, pl.ds(level, 1)])
            v_y = d_cross(
                v, rrecv[k, 0, pl.ds(levels + level, 1)], rrecv[k, 1, pl.ds(levels + level, 1)]
            )
            p_z = po[level + 2] - po[level]
            w_z = wo[level + 2] - wo[level]
            fresh = (
                advect * p_x + squared * (u_x + v_y + w_z),
                advect * u_x + half_step * p_x,
                advect * v_x + half_step * p_y,
                advect * w_x + half_step * p_z,
            )
            new = []
            for field, (rate, old) in enumerate(zip(fresh, (p, u, v, w))):
                change = -rate if section == 0 else keep * chg[field, level] - rate
                if section < 2:
                    chg[field, level] = change
                new.append(old + gain * change)
            if last:
                for field in range(4):
                    out_ref[field, level] = new[field]
            else:
                pn[level + 1], un[level], vn[level], wn[level + 1] = new
                for field, value in ((0, new[0]), (1, new[2])):
                    rsend[k + 1, 0, pl.ds(field * levels + level, 1)] = value[0:1]
                    rsend[k + 1, 1, pl.ds(field * levels + level, 1)] = value[rows - 1 : rows]
            return carry

        lax.fori_loop(0, levels, update, 0)
        if not last:
            send_rows(k + 1)
            send_levels(k + 1, pn, wn)

    def left(k, carry):
        gather_copy(k).wait_send()
        for step in range(steps):
            spread_copy(step, k).wait_send()
        return carry

    lax.fori_loop(1, n, left, 0)
    for k in range(sections):
        for side, there in ((0, has_left), (1, has_right)):
            @pl.when(there)
            def _():
                row_copy(k, side).wait_send()
        for side, there in ((0, has_below), (1, has_above)):
            @pl.when(there)
            def _():
                level_copy(k, side).wait_send()


def body(n, floors, state, turbulence, wind, ground_admittance, ground_kind, drift_cells, drift_eighths):
    fields, levels, rows, cols = state.shape
    steps = drift_cells.shape[0]
    sections = 3 * steps
    width = 2 * levels * cols // n
    f32, bf16 = jnp.float32, jnp.bfloat16
    padded = pltpu.VMEM((levels + 2, rows, cols), f32)
    plain = pltpu.VMEM((levels, rows, cols), f32)
    dma = pltpu.SemaphoreType.DMA
    vmem = pl.BlockSpec(memory_space=pltpu.VMEM)
    smem = pl.BlockSpec(memory_space=pltpu.SMEM)
    hbm = pl.BlockSpec(memory_space=pl.ANY)
    return pl.pallas_call(
        functools.partial(kernel, n, floors, steps, levels, rows, cols, width),
        out_shape=jax.ShapeDtypeStruct(state.shape, f32),
        in_specs=[hbm, vmem, smem, vmem, vmem, smem, smem],
        out_specs=vmem,
        scratch_shapes=[
            padded, plain, plain, padded,
            padded, plain, plain, padded,
            pltpu.VMEM((fields, levels, rows, cols), f32),
            plain,
            plain,
            pltpu.VMEM((n * rows, width), bf16),
            pltpu.VMEM((steps, n * rows, width), bf16),
            pltpu.VMEM((steps, 2, levels, rows, cols), bf16),
            pltpu.VMEM((sections, 2, 2 * levels, cols), f32),
            pltpu.VMEM((sections, 2, 2 * levels, cols), f32),
            pltpu.VMEM((sections, 2, 2, rows, cols), bf16),
            pltpu.VMEM((sections, 2, 2, rows, cols), bf16),
            dma((5,)),
            dma((n,)), dma((n,)),
            dma((steps, n)), dma((steps, n)),
            dma((sections, 2)), dma((sections, 2)),
            dma((sections, 2)), dma((sections, 2)),
        ],
        compiler_params=pltpu.CompilerParams(
            collective_id=0, has_side_effects=True, vmem_limit_bytes=40 * 2**20
        ),
    )(state, turbulence, wind, ground_admittance, ground_kind, drift_cells, drift_eighths)


def solution(mesh):
    placed = (
        P(None, "height", "cross", None),
        P(None, "height", "cross", None),
        P("height"),
        P("cross", None),
        P("cross", None),
        P(None, "height"),
        P(None, "height"),
    )
    return jax.shard_map(
        functools.partial(body, mesh.shape["cross"], mesh.shape["height"]),
        mesh=mesh,
        in_specs=placed,
        out_specs=P(None, "height", "cross", None),
        check_vma=False,
    )
```

```python
import functools
import math

import jax
import jax.numpy as jnp
from jax import lax
from jax.experimental import pallas as pl
from jax.experimental.pallas import tpu as pltpu
from jax.sharding import PartitionSpec as P

section_keep = (0.0, -5.0 / 9.0, -153.0 / 128.0)
section_gain = (1.0 / 3.0, 15.0 / 16.0, 8.0 / 15.0)
time_step = 0.4
half_step = 0.5 * time_step
MESH = pl.DeviceIdType.MESH


def kernel(
    n, floors, steps, levels, rows, cols, width,
    state_ref, turb_ref, wind_in, adm_in, kind_in, cells_in, eighths_in,
    out_ref,
    wind_ref, adm_ref, kind_ref, cells_ref, eighths_ref,
    pa, ua, va, wa, pb, ub, vb, wb, chg, adv, sqr, gath, outb, froz,
    rsend, rrecv, hsend, hrecv,
    in_sem, out_sem, s1, r1, s2, r2, rs, rr, hs, hr,
):
    me = lax.axis_index("cross")
    floor = lax.axis_index("height")
    length = n * rows
    pieces = cols // width
    sections = 3 * steps
    half = levels // 2

    def part(j):
        field = j // (levels * pieces)
        rest = j % (levels * pieces)
        return field, rest // pieces, pl.multiple_of((rest % pieces) * width, width)

    def peer(k):
        return lax.rem(me + k, n)

    def rows_of(j):
        return pl.ds(pl.multiple_of(j * rows, rows), rows)

    has_left, has_right = me > 0, me < n - 1
    has_below, has_above = floor > 0, floor < floors - 1

    loads = [
        pltpu.make_async_copy(state_ref.at[0], pa.at[pl.ds(1, levels)], in_sem.at[0]),
        pltpu.make_async_copy(state_ref.at[1], ua, in_sem.at[1]),
        pltpu.make_async_copy(state_ref.at[2], va, in_sem.at[2]),
        pltpu.make_async_copy(state_ref.at[3], wa.at[pl.ds(1, levels)], in_sem.at[3]),
        pltpu.make_async_copy(wind_in, wind_ref, in_sem.at[5]),
        pltpu.make_async_copy(adm_in, adm_ref, in_sem.at[6]),
        pltpu.make_async_copy(kind_in, kind_ref, in_sem.at[7]),
        pltpu.make_async_copy(cells_in, cells_ref, in_sem.at[8]),
        pltpu.make_async_copy(eighths_in, eighths_ref, in_sem.at[9]),
    ]
    for load in loads:
        load.start()

    barrier = pltpu.get_barrier_semaphore()

    def greet(k, carry):
        pl.semaphore_signal(barrier, inc=1, device_id={"cross": peer(k)}, device_id_type=MESH)
        return carry

    lax.fori_loop(1, n, greet, 0)

    @pl.when(has_below)
    def _():
        pl.semaphore_signal(barrier, inc=1, device_id={"height": floor - 1}, device_id_type=MESH)

    @pl.when(has_above)
    def _():
        pl.semaphore_signal(barrier, inc=1, device_id={"height": floor + 1}, device_id_type=MESH)

    zero_rows = jnp.zeros((2 * levels, cols), jnp.float32)
    for k in range(sections):
        @pl.when(jnp.logical_not(has_left))
        def _():
            rrecv[k, 0] = zero_rows

        @pl.when(jnp.logical_not(has_right))
        def _():
            rrecv[k, 1] = zero_rows

    pl.semaphore_wait(
        barrier, n - 1 + has_below.astype(jnp.int32) + has_above.astype(jnp.int32)
    )

    def gather_copy(k):
        to = peer(k)
        field, level, at = part(to)
        return pltpu.make_async_remote_copy(
            src_ref=turb_ref.at[field, level, :, pl.ds(at, width)],
            dst_ref=gath.at[rows_of(me)],
            send_sem=s1.at[to],
            recv_sem=r1.at[me],
            device_id={"cross": to},
            device_id_type=MESH,
        )

    def gather_wait(k):
        source = peer(k)
        return pltpu.make_async_remote_copy(
            src_ref=gath.at[rows_of(source)],
            dst_ref=gath.at[rows_of(source)],
            send_sem=s1.at[source],
            recv_sem=r1.at[source],
            device_id={"cross": source},
            device_id_type=MESH,
        )

    def start_gather(k, carry):
        gather_copy(k).start()
        return carry

    lax.fori_loop(1, n, start_gather, 0)
    my_field, my_level, my_at = part(me)
    own = pltpu.make_async_copy(
        turb_ref.at[my_field, my_level, :, pl.ds(my_at, width)], gath.at[rows_of(me)], in_sem.at[4]
    )
    own.start()

    def row_copy(k, side, group):
        to = me - 1 if side == 0 else me + 1
        lines = pl.ds(2 * half * group, 2 * half)
        return pltpu.make_async_remote_copy(
            src_ref=rsend.at[k, side, lines],
            dst_ref=rrecv.at[k, 1 - side, lines],
            send_sem=rs.at[k, side, group],
            recv_sem=rr.at[k, 1 - side, group],
            device_id={"cross": to},
            device_id_type=MESH,
        )

    def level_copy(k, side):
        to = floor - 1 if side == 0 else floor + 1
        return pltpu.make_async_remote_copy(
            src_ref=hsend.at[k, side],
            dst_ref=hrecv.at[k, 1 - side],
            send_sem=hs.at[k, side],
            recv_sem=hr.at[k, 1 - side],
            device_id={"height": to},
            device_id_type=MESH,
        )

    def send_rows(k, group):
        @pl.when(has_left)
        def _():
            row_copy(k, 0, group).start()

        @pl.when(has_right)
        def _():
            row_copy(k, 1, group).start()

    def receive_rows(k, group):
        @pl.when(has_left)
        def _():
            row_copy(k, 1, group).wait_recv()

        @pl.when(has_right)
        def _():
            row_copy(k, 0, group).wait_recv()

    def send_down(k, pn, wn):
        @pl.when(has_below)
        def _():
            hsend[k, 0, 0] = pn[1].astype(jnp.bfloat16)
            hsend[k, 0, 1] = wn[1].astype(jnp.bfloat16)
            level_copy(k, 0).start()

    def send_up(k, pn, wn):
        @pl.when(has_above)
        def _():
            hsend[k, 1, 0] = pn[levels].astype(jnp.bfloat16)
            hsend[k, 1, 1] = wn[levels].astype(jnp.bfloat16)
            level_copy(k, 1).start()

    def receive_below(k, pn, wn):
        @pl.when(has_below)
        def _():
            level_copy(k, 1).wait_recv()
            pn[0] = hrecv[k, 0, 0].astype(jnp.float32)
            wn[0] = hrecv[k, 0, 1].astype(jnp.float32)

        @pl.when(jnp.logical_not(has_below))
        def _():
            ground = 2.0 * adm_ref[...] * kind_ref[...].astype(jnp.float32)
            low = pn[1]
            pn[0] = low
            wn[0] = ground * low - wn[1]

    def receive_above(k, pn, wn):
        @pl.when(has_above)
        def _():
            level_copy(k, 0).wait_recv()
            pn[levels + 1] = hrecv[k, 1, 0].astype(jnp.float32)
            wn[levels + 1] = hrecv[k, 1, 1].astype(jnp.float32)

        @pl.when(jnp.logical_not(has_above))
        def _():
            pn[levels + 1] = jnp.zeros((rows, cols), jnp.float32)
            wn[levels + 1] = jnp.zeros((rows, cols), jnp.float32)

    for load in loads:
        load.wait()

    def first_rows(level, carry):
        for field, ref, offset in ((0, pa, 1), (1, va, 0)):
            rsend[0, 0, pl.ds(2 * level + field, 1)] = ref[level + offset, pl.ds(0, 1)]
            rsend[0, 1, pl.ds(2 * level + field, 1)] = ref[level + offset, pl.ds(rows - 1, 1)]
        return carry

    lax.fori_loop(0, levels, first_rows, 0)
    send_down(0, pa, wa)
    send_rows(0, 0)
    send_up(0, pa, wa)
    send_rows(0, 1)

    own.wait()

    def whole(k, carry):
        gather_wait(k).wait_recv()
        return carry

    lax.fori_loop(1, n, whole, 0)
    block = math.gcd(length, 256)

    def spread_copy(step, k):
        to = peer(k)
        return pltpu.make_async_remote_copy(
            src_ref=outb.at[step, rows_of(to)],
            dst_ref=froz.at[step, my_field, my_level, :, pl.ds(my_at, width)],
            send_sem=s2.at[step, to],
            recv_sem=r2.at[step, me],
            device_id={"cross": to},
            device_id_type=MESH,
        )

    def spread_wait(step, k):
        source = peer(k)
        field, level, at = part(source)
        return pltpu.make_async_remote_copy(
            src_ref=outb.at[step, rows_of(source)],
            dst_ref=froz.at[step, field, level, :, pl.ds(at, width)],
            send_sem=s2.at[step, source],
            recv_sem=r2.at[step, source],
            device_id={"cross": source},
            device_id_type=MESH,
        )

    def spread_some(step, third, of):
        def spread(k, carry):
            spread_copy(step, k).start()
            return carry

        lax.fori_loop(1 + (n - 1) * third // of, 1 + (n - 1) * (third + 1) // of, spread, 0)

    for step in range(steps):
        cells = cells_ref[step, my_level]
        weight = eighths_ref[step, my_level].astype(jnp.float32) / 8.0

        def mix(i, carry, step=step, cells=cells, weight=weight):
            top = pl.multiple_of(i * block, block)
            to_row = lax.broadcasted_iota(jnp.int32, (block, length), 0) + top
            from_row = lax.broadcasted_iota(jnp.int32, (block, length), 1)
            back = to_row - from_row - cells
            back = jnp.where(back < 0, back + length, back)
            back = jnp.where(back < 0, back + length, back)
            share = jnp.where(back == 0, 1.0 - weight, jnp.where(back == 1, weight, 0.0))
            outb[step, pl.ds(top, block)] = jnp.dot(
                share.astype(jnp.bfloat16), gath[...], preferred_element_type=jnp.float32
            ).astype(jnp.bfloat16)
            return carry

        lax.fori_loop(0, length // block, mix, 0)

        if step == 0:
            spread_some(0, 0, 1)
        froz[step, my_field, my_level, :, pl.ds(my_at, width)] = outb[step, rows_of(me)]

    row_id = lax.broadcasted_iota(jnp.int32, (rows, cols), 0)
    col_id = lax.broadcasted_iota(jnp.int32, (rows, cols), 1)

    def d_range(f):
        ahead = jnp.where(col_id == cols - 1, 0.0, pltpu.roll(f, cols - 1, 1))
        behind = jnp.where(col_id == 0, 0.0, pltpu.roll(f, 1, 1))
        return ahead - behind

    def d_cross(f, before, after):
        ahead = jnp.where(row_id == rows - 1, after, pltpu.roll(f, rows - 1, 0))
        behind = jnp.where(row_id == 0, before, pltpu.roll(f, 1, 0))
        return ahead - behind

    def out_copy(level):
        return pltpu.make_async_copy(chg.at[:, level], out_ref.at[:, level], out_sem.at[level])

    sets = ((pa, ua, va, wa), (pb, ub, vb, wb))
    for k in range(sections):
        step, section = k // 3, k % 3
        po, uo, vo, wo = sets[k % 2]
        pn, un, vn, wn = sets[(k + 1) % 2]
        last = k == sections - 1
        if section == 0:
            def arrive(j, carry, step=step):
                spread_wait(step, j).wait_recv()
                return carry

            lax.fori_loop(1, n, arrive, 0)
        if step + 1 < steps:
            spread_some(step + 1, section, 3)
        receive_below(k, po, wo)
        receive_rows(k, 0)
        keep, gain = section_keep[section], section_gain[section]

        def update(i, carry):
            level = jnp.where(i < half, i, jnp.where(i == half, levels - 1, i - 1))

            @pl.when(i == half)
            def _():
                receive_above(k, po, wo)
                receive_rows(k, 1)

            if section == 0:
                frozen = froz[step, 0, level].astype(jnp.float32)
                speed = 1.0 + froz[step, 1, level].astype(jnp.float32)
                advect = half_step * (wind_ref[level] + frozen)
                squared = half_step * (speed * speed)
                adv[level] = advect
                sqr[level] = squared
            else:
                advect = adv[level]
                squared = sqr[level]
            p, u, v, w = po[level + 1], uo[level], vo[level], wo[level + 1]
            p_x, u_x, v_x, w_x = d_range(p), d_range(u), d_range(v), d_range(w)
            p_y = d_cross(p, rrecv[k, 0, pl.ds(2 * level, 1)], rrecv[k, 1, pl.ds(2 * level, 1)])
            v_y = d_cross(
                v, rrecv[k, 0, pl.ds(2 * level + 1, 1)], rrecv[k, 1, pl.ds(2 * level + 1, 1)]
            )
            p_z = po[level + 2] - po[level]
            w_z = wo[level + 2] - wo[level]
            fresh = (
                advect * p_x + squared * (u_x + v_y + w_z),
                advect * u_x + half_step * p_x,
                advect * v_x + half_step * p_y,
                advect * w_x + half_step * p_z,
            )
            new = []
            for field, (rate, old) in enumerate(zip(fresh, (p, u, v, w))):
                change = -rate if section == 0 else keep * chg[field, level] - rate
                if section < 2:
                    chg[field, level] = change
                new.append(old + gain * change)
            if last:
                for field in range(4):
                    chg[field, level] = new[field]
                out_copy(level).start()
            else:
                pn[level + 1], un[level], vn[level], wn[level + 1] = new
                for field, value in ((0, new[0]), (1, new[2])):
                    rsend[k + 1, 0, pl.ds(2 * level + field, 1)] = value[0:1]
                    rsend[k + 1, 1, pl.ds(2 * level + field, 1)] = value[rows - 1 : rows]

                @pl.when(i == 0)
                def _():
                    send_down(k + 1, pn, wn)

                @pl.when(i == half - 1)
                def _():
                    send_rows(k + 1, 0)

                @pl.when(i == half)
                def _():
                    send_up(k + 1, pn, wn)

            return carry

        lax.fori_loop(0, levels, update, 0)
        if not last:
            send_rows(k + 1, 1)

    def stored(level, carry):
        out_copy(level).wait()
        return carry

    lax.fori_loop(0, levels, stored, 0)

    def left(k, carry):
        gather_copy(k).wait_send()
        for step in range(steps):
            spread_copy(step, k).wait_send()
        return carry

    lax.fori_loop(1, n, left, 0)
    for k in range(sections):
        for side, there in ((0, has_left), (1, has_right)):
            @pl.when(there)
            def _():
                row_copy(k, side, 0).wait_send()
                row_copy(k, side, 1).wait_send()
        for side, there in ((0, has_below), (1, has_above)):
            @pl.when(there)
            def _():
                level_copy(k, side).wait_send()


def body(n, floors, state, turbulence, wind, ground_admittance, ground_kind, drift_cells, drift_eighths):
    fields, levels, rows, cols = state.shape
    steps = drift_cells.shape[0]
    sections = 3 * steps
    width = 2 * levels * cols // n
    f32, bf16 = jnp.float32, jnp.bfloat16
    padded = pltpu.VMEM((levels + 2, rows, cols), f32)
    plain = pltpu.VMEM((levels, rows, cols), f32)
    dma = pltpu.SemaphoreType.DMA
    hbm = pl.BlockSpec(memory_space=pl.ANY)
    return pl.pallas_call(
        functools.partial(kernel, n, floors, steps, levels, rows, cols, width),
        out_shape=jax.ShapeDtypeStruct(state.shape, f32),
        in_specs=[hbm] * 7,
        out_specs=hbm,
        scratch_shapes=[
            pltpu.SMEM((levels,), f32),
            pltpu.VMEM((rows, cols), f32),
            pltpu.VMEM((rows, cols), jnp.int32),
            pltpu.SMEM((steps, levels), jnp.int32),
            pltpu.SMEM((steps, levels), jnp.int32),
            padded, plain, plain, padded,
            padded, plain, plain, padded,
            pltpu.VMEM((fields, levels, rows, cols), f32),
            plain,
            plain,
            pltpu.VMEM((n * rows, width), bf16),
            pltpu.VMEM((steps, n * rows, width), bf16),
            pltpu.VMEM((steps, 2, levels, rows, cols), bf16),
            pltpu.VMEM((sections, 2, 2 * levels, cols), f32),
            pltpu.VMEM((sections, 2, 2 * levels, cols), f32),
            pltpu.VMEM((sections, 2, 2, rows, cols), bf16),
            pltpu.VMEM((sections, 2, 2, rows, cols), bf16),
            dma((10,)), dma((levels,)),
            dma((n,)), dma((n,)),
            dma((steps, n)), dma((steps, n)),
            dma((sections, 2, 2)), dma((sections, 2, 2)),
            dma((sections, 2)), dma((sections, 2)),
        ],
        compiler_params=pltpu.CompilerParams(
            collective_id=0, has_side_effects=True, vmem_limit_bytes=60 * 2**20
        ),
    )(state, turbulence, wind, ground_admittance, ground_kind, drift_cells, drift_eighths)


def solution(mesh):
    placed = (
        P(None, "height", "cross", None),
        P(None, "height", "cross", None),
        P("height"),
        P("cross", None),
        P("cross", None),
        P(None, "height"),
        P(None, "height"),
    )
    return jax.shard_map(
        functools.partial(body, mesh.shape["cross"], mesh.shape["height"]),
        mesh=mesh,
        in_specs=placed,
        out_specs=P(None, "height", "cross", None),
        check_vma=False,
    )
```

```python
import functools
import math

import jax
import jax.numpy as jnp
from jax import lax
from jax.experimental import pallas as pl
from jax.experimental.pallas import tpu as pltpu
from jax.sharding import PartitionSpec as P

section_keep = (0.0, -5.0 / 9.0, -153.0 / 128.0)
section_gain = (1.0 / 3.0, 15.0 / 16.0, 8.0 / 15.0)
time_step = 0.4
half_step = 0.5 * time_step
MESH = pl.DeviceIdType.MESH


def kernel(
    n, floors, steps, levels, rows, cols, width,
    state_ref, turb_ref, wind_in, adm_in, kind_in, cells_in, eighths_in,
    out_ref,
    wind_ref, adm_ref, kind_ref, cells_ref, eighths_ref,
    pa, ua, va, wa, pb, ub, vb, wb, chg, adv, sqr, gath, share, outb, froz,
    rsend, rrecv, hsend, hrecv,
    in_sem, out_sem, s1, r1, s2, r2, rs, rr, hs, hr,
):
    me = lax.axis_index("cross")
    floor = lax.axis_index("height")
    length = n * rows
    pieces = cols // width
    sections = 3 * steps
    half = levels // 2

    def part(j):
        field = jnp.where(j >= levels * pieces, 1, 0)
        rest = j - field * (levels * pieces)
        if pieces == 1:
            return field, rest, 0
        level = lax.div(rest, pieces)
        return field, level, pl.multiple_of((rest - level * pieces) * width, width)

    def peer(k):
        j = me + k
        return jnp.where(j >= n, j - n, j)

    def rows_of(j):
        return pl.ds(pl.multiple_of(j * rows, rows), rows)

    has_left, has_right = me > 0, me < n - 1
    has_below, has_above = floor > 0, floor < floors - 1

    loads = [
        pltpu.make_async_copy(state_ref.at[0], pa.at[pl.ds(1, levels)], in_sem.at[0]),
        pltpu.make_async_copy(state_ref.at[1], ua, in_sem.at[1]),
        pltpu.make_async_copy(state_ref.at[2], va, in_sem.at[2]),
        pltpu.make_async_copy(state_ref.at[3], wa.at[pl.ds(1, levels)], in_sem.at[3]),
        pltpu.make_async_copy(wind_in, wind_ref, in_sem.at[5]),
        pltpu.make_async_copy(adm_in, adm_ref, in_sem.at[6]),
        pltpu.make_async_copy(kind_in, kind_ref, in_sem.at[7]),
        pltpu.make_async_copy(cells_in, cells_ref, in_sem.at[8]),
        pltpu.make_async_copy(eighths_in, eighths_ref, in_sem.at[9]),
    ]
    for load in loads:
        load.start()

    barrier = pltpu.get_barrier_semaphore()

    def greet(k, carry):
        pl.semaphore_signal(barrier, inc=1, device_id={"cross": peer(k)}, device_id_type=MESH)
        return carry

    lax.fori_loop(1, n, greet, 0)

    @pl.when(has_below)
    def _():
        pl.semaphore_signal(barrier, inc=1, device_id={"height": floor - 1}, device_id_type=MESH)

    @pl.when(has_above)
    def _():
        pl.semaphore_signal(barrier, inc=1, device_id={"height": floor + 1}, device_id_type=MESH)

    zero_rows = jnp.zeros((2 * levels, cols), jnp.float32)
    for k in range(sections):
        @pl.when(jnp.logical_not(has_left))
        def _():
            rrecv[k, 0] = zero_rows

        @pl.when(jnp.logical_not(has_right))
        def _():
            rrecv[k, 1] = zero_rows

    pl.semaphore_wait(
        barrier, n - 1 + has_below.astype(jnp.int32) + has_above.astype(jnp.int32)
    )

    def gather_copy(k):
        to = peer(k)
        field, level, at = part(to)
        return pltpu.make_async_remote_copy(
            src_ref=turb_ref.at[field, level, :, pl.ds(at, width)],
            dst_ref=gath.at[rows_of(me)],
            send_sem=s1,
            recv_sem=r1,
            device_id={"cross": to},
            device_id_type=MESH,
        )

    all_but_one = pl.ds(0, (n - 1) * rows)

    def gather_all():
        return pltpu.make_async_remote_copy(
            src_ref=gath.at[all_but_one],
            dst_ref=gath.at[all_but_one],
            send_sem=s1,
            recv_sem=r1,
            device_id={"cross": peer(1)},
            device_id_type=MESH,
        )

    def spread_all(step):
        return pltpu.make_async_remote_copy(
            src_ref=outb.at[step, all_but_one],
            dst_ref=outb.at[step, all_but_one],
            send_sem=s2.at[step],
            recv_sem=r2.at[step],
            device_id={"cross": peer(1)},
            device_id_type=MESH,
        )

    def start_gather(k, carry):
        gather_copy(k).start()
        return carry

    lax.fori_loop(1, n, start_gather, 0)
    my_field, my_level, my_at = part(me)
    own = pltpu.make_async_copy(
        turb_ref.at[my_field, my_level, :, pl.ds(my_at, width)], gath.at[rows_of(me)], in_sem.at[4]
    )
    own.start()

    def row_copy(k, side, group):
        to = me - 1 if side == 0 else me + 1
        lines = pl.ds(2 * half * group, 2 * half)
        return pltpu.make_async_remote_copy(
            src_ref=rsend.at[k, side, lines],
            dst_ref=rrecv.at[k, 1 - side, lines],
            send_sem=rs.at[k, side, group],
            recv_sem=rr.at[k, 1 - side, group],
            device_id={"cross": to},
            device_id_type=MESH,
        )

    def level_copy(k, side):
        to = floor - 1 if side == 0 else floor + 1
        return pltpu.make_async_remote_copy(
            src_ref=hsend.at[k, side],
            dst_ref=hrecv.at[k, 1 - side],
            send_sem=hs.at[k, side],
            recv_sem=hr.at[k, 1 - side],
            device_id={"height": to},
            device_id_type=MESH,
        )

    def send_rows(k, group):
        @pl.when(has_left)
        def _():
            row_copy(k, 0, group).start()

        @pl.when(has_right)
        def _():
            row_copy(k, 1, group).start()

    def receive_rows(k, group):
        @pl.when(has_left)
        def _():
            row_copy(k, 1, group).wait_recv()

        @pl.when(has_right)
        def _():
            row_copy(k, 0, group).wait_recv()

    def send_down(k, pn, wn):
        @pl.when(has_below)
        def _():
            hsend[k, 0, 0] = pn[1].astype(jnp.bfloat16)
            hsend[k, 0, 1] = wn[1].astype(jnp.bfloat16)
            level_copy(k, 0).start()

    def send_up(k, pn, wn):
        @pl.when(has_above)
        def _():
            hsend[k, 1, 0] = pn[levels].astype(jnp.bfloat16)
            hsend[k, 1, 1] = wn[levels].astype(jnp.bfloat16)
            level_copy(k, 1).start()

    def receive_below(k, pn, wn):
        @pl.when(has_below)
        def _():
            level_copy(k, 1).wait_recv()
            pn[0] = hrecv[k, 0, 0].astype(jnp.float32)
            wn[0] = hrecv[k, 0, 1].astype(jnp.float32)

        @pl.when(jnp.logical_not(has_below))
        def _():
            ground = 2.0 * adm_ref[...] * kind_ref[...].astype(jnp.float32)
            low = pn[1]
            pn[0] = low
            wn[0] = ground * low - wn[1]

    def receive_above(k, pn, wn):
        @pl.when(has_above)
        def _():
            level_copy(k, 0).wait_recv()
            pn[levels + 1] = hrecv[k, 1, 0].astype(jnp.float32)
            wn[levels + 1] = hrecv[k, 1, 1].astype(jnp.float32)

        @pl.when(jnp.logical_not(has_above))
        def _():
            pn[levels + 1] = jnp.zeros((rows, cols), jnp.float32)
            wn[levels + 1] = jnp.zeros((rows, cols), jnp.float32)

    for load in loads:
        load.wait()

    def first_rows(level, carry):
        for field, ref, offset in ((0, pa, 1), (1, va, 0)):
            rsend[0, 0, pl.ds(2 * level + field, 1)] = ref[level + offset, pl.ds(0, 1)]
            rsend[0, 1, pl.ds(2 * level + field, 1)] = ref[level + offset, pl.ds(rows - 1, 1)]
        return carry

    lax.fori_loop(0, levels, first_rows, 0)
    send_down(0, pa, wa)
    send_rows(0, 0)
    send_up(0, pa, wa)
    send_rows(0, 1)


    block = math.gcd(length, 256)

    for step in range(steps):
        cells = cells_ref[step, my_level]
        weight = eighths_ref[step, my_level].astype(jnp.float32) / 8.0

        def weigh(i, carry, step=step, cells=cells, weight=weight):
            top = pl.multiple_of(i * block, block)
            to_row = lax.broadcasted_iota(jnp.int32, (block, length), 0) + top
            from_row = lax.broadcasted_iota(jnp.int32, (block, length), 1)
            back = to_row - from_row - cells
            back = jnp.where(back < 0, back + length, back)
            back = jnp.where(back < 0, back + length, back)
            mix = jnp.where(back == 0, 1.0 - weight, jnp.where(back == 1, weight, 0.0))
            share[step, pl.ds(top, block)] = mix.astype(jnp.bfloat16)
            return carry

        lax.fori_loop(0, length // block, weigh, 0)

    own.wait()
    gather_all().wait_recv()

    def spread_copy(step, k):
        to = peer(k)
        return pltpu.make_async_remote_copy(
            src_ref=outb.at[step, rows_of(to)],
            dst_ref=froz.at[step, my_field, my_level, :, pl.ds(my_at, width)],
            send_sem=s2.at[step],
            recv_sem=r2.at[step],
            device_id={"cross": to},
            device_id_type=MESH,
        )

    def spread_some(step, third, of):
        def spread(k, carry):
            spread_copy(step, k).start()
            return carry

        lax.fori_loop(1 + (n - 1) * third // of, 1 + (n - 1) * (third + 1) // of, spread, 0)

    for step in range(steps):
        def mix(i, carry, step=step):
            top = pl.multiple_of(i * block, block)
            outb[step, pl.ds(top, block)] = jnp.dot(
                share[step, pl.ds(top, block)], gath[...], preferred_element_type=jnp.float32
            ).astype(jnp.bfloat16)
            return carry

        lax.fori_loop(0, length // block, mix, 0)

        if step == 0:
            spread_some(0, 0, 1)
        froz[step, my_field, my_level, :, pl.ds(my_at, width)] = outb[step, rows_of(me)]

    row_id = lax.broadcasted_iota(jnp.int32, (rows, cols), 0)
    col_id = lax.broadcasted_iota(jnp.int32, (rows, cols), 1)

    def d_range(f):
        ahead = jnp.where(col_id == cols - 1, 0.0, pltpu.roll(f, cols - 1, 1))
        behind = jnp.where(col_id == 0, 0.0, pltpu.roll(f, 1, 1))
        return ahead - behind

    def d_cross(f, before, after):
        ahead = jnp.where(row_id == rows - 1, after, pltpu.roll(f, rows - 1, 0))
        behind = jnp.where(row_id == 0, before, pltpu.roll(f, 1, 0))
        return ahead - behind

    def out_copy(level):
        return pltpu.make_async_copy(chg.at[:, level], out_ref.at[:, level], out_sem.at[level])

    sets = ((pa, ua, va, wa), (pb, ub, vb, wb))
    for k in range(sections):
        step, section = k // 3, k % 3
        po, uo, vo, wo = sets[k % 2]
        pn, un, vn, wn = sets[(k + 1) % 2]
        last = k == sections - 1
        if section == 0:
            spread_all(step).wait_recv()
        if step + 1 < steps:
            spread_some(step + 1, section, 3)
        receive_below(k, po, wo)
        receive_rows(k, 0)
        keep, gain = section_keep[section], section_gain[section]

        def update(i, carry):
            level = jnp.where(i < half, i, jnp.where(i == half, levels - 1, i - 1))

            @pl.when(i == half)
            def _():
                receive_above(k, po, wo)
                receive_rows(k, 1)

            if section == 0:
                frozen = froz[step, 0, level].astype(jnp.float32)
                speed = 1.0 + froz[step, 1, level].astype(jnp.float32)
                advect = half_step * (wind_ref[level] + frozen)
                squared = half_step * (speed * speed)
                adv[level] = advect
                sqr[level] = squared
            else:
                advect = adv[level]
                squared = sqr[level]
            p, u, v, w = po[level + 1], uo[level], vo[level], wo[level + 1]
            p_x, u_x, v_x, w_x = d_range(p), d_range(u), d_range(v), d_range(w)
            p_y = d_cross(p, rrecv[k, 0, pl.ds(2 * level, 1)], rrecv[k, 1, pl.ds(2 * level, 1)])
            v_y = d_cross(
                v, rrecv[k, 0, pl.ds(2 * level + 1, 1)], rrecv[k, 1, pl.ds(2 * level + 1, 1)]
            )
            p_z = po[level + 2] - po[level]
            w_z = wo[level + 2] - wo[level]
            fresh = (
                advect * p_x + squared * (u_x + v_y + w_z),
                advect * u_x + half_step * p_x,
                advect * v_x + half_step * p_y,
                advect * w_x + half_step * p_z,
            )
            new = []
            for field, (rate, old) in enumerate(zip(fresh, (p, u, v, w))):
                change = -rate if section == 0 else keep * chg[field, level] - rate
                if section < 2:
                    chg[field, level] = change
                new.append(old + gain * change)
            if last:
                for field in range(4):
                    chg[field, level] = new[field]
                out_copy(level).start()
            else:
                pn[level + 1], un[level], vn[level], wn[level + 1] = new
                for field, value in ((0, new[0]), (1, new[2])):
                    rsend[k + 1, 0, pl.ds(2 * level + field, 1)] = value[0:1]
                    rsend[k + 1, 1, pl.ds(2 * level + field, 1)] = value[rows - 1 : rows]

                @pl.when(i == 0)
                def _():
                    send_down(k + 1, pn, wn)

                @pl.when(i == half - 1)
                def _():
                    send_rows(k + 1, 0)

                @pl.when(i == half)
                def _():
                    send_up(k + 1, pn, wn)

            return carry

        lax.fori_loop(0, levels, update, 0)
        if not last:
            send_rows(k + 1, 1)

    def stored(level, carry):
        out_copy(level).wait()
        return carry

    lax.fori_loop(0, levels, stored, 0)

    gather_all().wait_send()
    for step in range(steps):
        spread_all(step).wait_send()
    for k in range(sections):
        for side, there in ((0, has_left), (1, has_right)):
            @pl.when(there)
            def _():
                row_copy(k, side, 0).wait_send()
                row_copy(k, side, 1).wait_send()
        for side, there in ((0, has_below), (1, has_above)):
            @pl.when(there)
            def _():
                level_copy(k, side).wait_send()


def body(n, floors, state, turbulence, wind, ground_admittance, ground_kind, drift_cells, drift_eighths):
    fields, levels, rows, cols = state.shape
    steps = drift_cells.shape[0]
    sections = 3 * steps
    width = 2 * levels * cols // n
    f32, bf16 = jnp.float32, jnp.bfloat16
    padded = pltpu.VMEM((levels + 2, rows, cols), f32)
    plain = pltpu.VMEM((levels, rows, cols), f32)
    dma = pltpu.SemaphoreType.DMA
    hbm = pl.BlockSpec(memory_space=pl.ANY)
    return pl.pallas_call(
        functools.partial(kernel, n, floors, steps, levels, rows, cols, width),
        out_shape=jax.ShapeDtypeStruct(state.shape, f32),
        in_specs=[hbm] * 7,
        out_specs=hbm,
        scratch_shapes=[
            pltpu.SMEM((levels,), f32),
            pltpu.VMEM((rows, cols), f32),
            pltpu.VMEM((rows, cols), jnp.int32),
            pltpu.SMEM((steps, levels), jnp.int32),
            pltpu.SMEM((steps, levels), jnp.int32),
            padded, plain, plain, padded,
            padded, plain, plain, padded,
            pltpu.VMEM((fields, levels, rows, cols), f32),
            plain,
            plain,
            pltpu.VMEM((n * rows, width), bf16),
            pltpu.VMEM((steps, n * rows, n * rows), bf16),
            pltpu.VMEM((steps, n * rows, width), bf16),
            pltpu.VMEM((steps, 2, levels, rows, cols), bf16),
            pltpu.VMEM((sections, 2, 2 * levels, cols), f32),
            pltpu.VMEM((sections, 2, 2 * levels, cols), f32),
            pltpu.VMEM((sections, 2, 2, rows, cols), bf16),
            pltpu.VMEM((sections, 2, 2, rows, cols), bf16),
            dma((10,)), dma((levels,)),
            dma, dma,
            dma((steps,)), dma((steps,)),
            dma((sections, 2, 2)), dma((sections, 2, 2)),
            dma((sections, 2)), dma((sections, 2)),
        ],
        compiler_params=pltpu.CompilerParams(
            collective_id=0, has_side_effects=True, vmem_limit_bytes=60 * 2**20
        ),
    )(state, turbulence, wind, ground_admittance, ground_kind, drift_cells, drift_eighths)


def solution(mesh):
    placed = (
        P(None, "height", "cross", None),
        P(None, "height", "cross", None),
        P("height"),
        P("cross", None),
        P("cross", None),
        P(None, "height"),
        P(None, "height"),
    )
    return jax.shard_map(
        functools.partial(body, mesh.shape["cross"], mesh.shape["height"]),
        mesh=mesh,
        in_specs=placed,
        out_specs=P(None, "height", "cross", None),
        check_vma=False,
    )
```

```python
import functools
import math

import jax
import jax.numpy as jnp
from jax import lax
from jax.experimental import pallas as pl
from jax.experimental.pallas import tpu as pltpu
from jax.sharding import PartitionSpec as P

section_keep = (0.0, -5.0 / 9.0, -153.0 / 128.0)
section_gain = (1.0 / 3.0, 15.0 / 16.0, 8.0 / 15.0)
time_step = 0.4
half_step = 0.5 * time_step
MESH = pl.DeviceIdType.MESH


def kernel(
    n, floors, steps, levels, rows, cols, width,
    state_ref, turb_ref, wind_in, adm_in, kind_in, cells_in, eighths_in,
    out_ref,
    wind_ref, adm_ref, kind_ref, cells_ref, eighths_ref,
    pa, ua, va, wa, pb, ub, vb, wb, chg, adv, sqr, gath, share, outb, froz,
    rsend, rrecv, hsend, hrecv,
    in_sem, out_sem, s1, r1, s2, r2, rs, rr, hs, hr,
):
    me = lax.axis_index("cross")
    floor = lax.axis_index("height")
    length = n * rows
    pieces = cols // width
    sections = 3 * steps
    half = levels // 2

    def part(j):
        field = jnp.where(j >= levels * pieces, 1, 0)
        rest = j - field * (levels * pieces)
        if pieces == 1:
            return field, rest, 0
        level = lax.div(rest, pieces)
        return field, level, pl.multiple_of((rest - level * pieces) * width, width)

    def peer(k):
        j = me + k
        return jnp.where(j >= n, j - n, j)

    def rows_of(j):
        return pl.ds(pl.multiple_of(j * rows, rows), rows)

    has_left, has_right = me > 0, me < n - 1
    has_below, has_above = floor > 0, floor < floors - 1

    loads = [
        pltpu.make_async_copy(state_ref.at[0], pa.at[pl.ds(1, levels)], in_sem.at[0]),
        pltpu.make_async_copy(state_ref.at[1], ua, in_sem.at[1]),
        pltpu.make_async_copy(state_ref.at[2], va, in_sem.at[2]),
        pltpu.make_async_copy(state_ref.at[3], wa.at[pl.ds(1, levels)], in_sem.at[3]),
        pltpu.make_async_copy(wind_in, wind_ref, in_sem.at[5]),
        pltpu.make_async_copy(adm_in, adm_ref, in_sem.at[6]),
        pltpu.make_async_copy(kind_in, kind_ref, in_sem.at[7]),
        pltpu.make_async_copy(cells_in, cells_ref, in_sem.at[8]),
        pltpu.make_async_copy(eighths_in, eighths_ref, in_sem.at[9]),
    ]
    for load in loads:
        load.start()

    barrier = pltpu.get_barrier_semaphore()

    def greet(k, carry):
        pl.semaphore_signal(barrier, inc=1, device_id={"cross": peer(k)}, device_id_type=MESH)
        return carry

    lax.fori_loop(1, n, greet, 0)

    @pl.when(has_below)
    def _():
        pl.semaphore_signal(barrier, inc=1, device_id={"height": floor - 1}, device_id_type=MESH)

    @pl.when(has_above)
    def _():
        pl.semaphore_signal(barrier, inc=1, device_id={"height": floor + 1}, device_id_type=MESH)

    zero_rows = jnp.zeros((2 * levels, cols), jnp.float32)
    for k in range(sections):
        @pl.when(jnp.logical_not(has_left))
        def _():
            rrecv[k, 0] = zero_rows

        @pl.when(jnp.logical_not(has_right))
        def _():
            rrecv[k, 1] = zero_rows

    pl.semaphore_wait(
        barrier, n - 1 + has_below.astype(jnp.int32) + has_above.astype(jnp.int32)
    )

    def gather_copy(k):
        to = peer(k)
        field, level, at = part(to)
        return pltpu.make_async_remote_copy(
            src_ref=turb_ref.at[field, level, :, pl.ds(at, width)],
            dst_ref=gath.at[rows_of(me)],
            send_sem=s1,
            recv_sem=r1,
            device_id={"cross": to},
            device_id_type=MESH,
        )

    all_but_one = pl.ds(0, (n - 1) * rows)

    def gather_all():
        return pltpu.make_async_remote_copy(
            src_ref=gath.at[all_but_one],
            dst_ref=gath.at[all_but_one],
            send_sem=s1,
            recv_sem=r1,
            device_id={"cross": peer(1)},
            device_id_type=MESH,
        )

    def spread_all(step):
        return pltpu.make_async_remote_copy(
            src_ref=outb.at[step, all_but_one],
            dst_ref=outb.at[step, all_but_one],
            send_sem=s2.at[step],
            recv_sem=r2.at[step],
            device_id={"cross": peer(1)},
            device_id_type=MESH,
        )

    def start_gather(k, carry):
        gather_copy(k).start()
        return carry

    lax.fori_loop(1, n, start_gather, 0)
    my_field, my_level, my_at = part(me)
    own = pltpu.make_async_copy(
        turb_ref.at[my_field, my_level, :, pl.ds(my_at, width)], gath.at[rows_of(me)], in_sem.at[4]
    )
    own.start()

    def row_copy(k, side, group):
        to = me - 1 if side == 0 else me + 1
        lines = pl.ds(2 * half * group, 2 * half)
        return pltpu.make_async_remote_copy(
            src_ref=rsend.at[k, side, lines],
            dst_ref=rrecv.at[k, 1 - side, lines],
            send_sem=rs.at[k, side, group],
            recv_sem=rr.at[k, 1 - side, group],
            device_id={"cross": to},
            device_id_type=MESH,
        )

    def level_copy(k, side):
        to = floor - 1 if side == 0 else floor + 1
        return pltpu.make_async_remote_copy(
            src_ref=hsend.at[k, side],
            dst_ref=hrecv.at[k, 1 - side],
            send_sem=hs.at[k, side],
            recv_sem=hr.at[k, 1 - side],
            device_id={"height": to},
            device_id_type=MESH,
        )

    def send_rows(k, group):
        @pl.when(has_left)
        def _():
            row_copy(k, 0, group).start()

        @pl.when(has_right)
        def _():
            row_copy(k, 1, group).start()

    def receive_rows(k, group):
        @pl.when(has_left)
        def _():
            row_copy(k, 1, group).wait_recv()

        @pl.when(has_right)
        def _():
            row_copy(k, 0, group).wait_recv()

    def send_down(k, pn, wn):
        @pl.when(has_below)
        def _():
            hsend[k, 0, 0] = pn[1].astype(jnp.bfloat16)
            hsend[k, 0, 1] = wn[1].astype(jnp.bfloat16)
            level_copy(k, 0).start()

    def send_up(k, pn, wn):
        @pl.when(has_above)
        def _():
            hsend[k, 1, 0] = pn[levels].astype(jnp.bfloat16)
            hsend[k, 1, 1] = wn[levels].astype(jnp.bfloat16)
            level_copy(k, 1).start()

    def receive_below(k, pn, wn):
        @pl.when(has_below)
        def _():
            level_copy(k, 1).wait_recv()
            pn[0] = hrecv[k, 0, 0].astype(jnp.float32)
            wn[0] = hrecv[k, 0, 1].astype(jnp.float32)

        @pl.when(jnp.logical_not(has_below))
        def _():
            ground = 2.0 * adm_ref[...] * kind_ref[...].astype(jnp.float32)
            low = pn[1]
            pn[0] = low
            wn[0] = ground * low - wn[1]

    def receive_above(k, pn, wn):
        @pl.when(has_above)
        def _():
            level_copy(k, 0).wait_recv()
            pn[levels + 1] = hrecv[k, 1, 0].astype(jnp.float32)
            wn[levels + 1] = hrecv[k, 1, 1].astype(jnp.float32)

        @pl.when(jnp.logical_not(has_above))
        def _():
            pn[levels + 1] = jnp.zeros((rows, cols), jnp.float32)
            wn[levels + 1] = jnp.zeros((rows, cols), jnp.float32)

    for load in loads:
        load.wait()

    def first_rows(level, carry):
        for field, ref, offset in ((0, pa, 1), (1, va, 0)):
            rsend[0, 0, pl.ds(2 * level + field, 1)] = ref[level + offset, pl.ds(0, 1)]
            rsend[0, 1, pl.ds(2 * level + field, 1)] = ref[level + offset, pl.ds(rows - 1, 1)]
        return carry

    lax.fori_loop(0, levels, first_rows, 0)
    send_down(0, pa, wa)
    send_rows(0, 0)
    send_up(0, pa, wa)
    send_rows(0, 1)


    block = math.gcd(length, 256)

    for step in range(steps):
        cells = cells_ref[step, my_level]
        weight = eighths_ref[step, my_level].astype(jnp.float32) / 8.0

        def weigh(i, carry, step=step, cells=cells, weight=weight):
            top = pl.multiple_of(i * block, block)
            to_row = lax.broadcasted_iota(jnp.int32, (block, length), 0) + top
            from_row = lax.broadcasted_iota(jnp.int32, (block, length), 1)
            back = to_row - from_row - cells
            back = jnp.where(back < 0, back + length, back)
            back = jnp.where(back < 0, back + length, back)
            mix = jnp.where(back == 0, 1.0 - weight, jnp.where(back == 1, weight, 0.0))
            share[step, pl.ds(top, block)] = mix.astype(jnp.bfloat16)
            return carry

        lax.fori_loop(0, length // block, weigh, 0)

    own.wait()
    gather_all().wait_recv()

    def spread_copy(step, k):
        to = peer(k)
        return pltpu.make_async_remote_copy(
            src_ref=outb.at[step, rows_of(to)],
            dst_ref=froz.at[step, my_field, my_level, :, pl.ds(my_at, width)],
            send_sem=s2.at[step],
            recv_sem=r2.at[step],
            device_id={"cross": to},
            device_id_type=MESH,
        )

    def spread_some(step, third, of):
        def spread(k, carry):
            spread_copy(step, k).start()
            return carry

        lax.fori_loop(1 + (n - 1) * third // of, 1 + (n - 1) * (third + 1) // of, spread, 0)

    for step in range(steps):
        def mix(i, carry, step=step):
            top = pl.multiple_of(i * block, block)
            outb[step, pl.ds(top, block)] = jnp.dot(
                share[step, pl.ds(top, block)], gath[...], preferred_element_type=jnp.float32
            ).astype(jnp.bfloat16)
            return carry

        lax.fori_loop(0, length // block, mix, 0)

        if step == 0:
            spread_some(0, 0, 1)
        froz[step, my_field, my_level, :, pl.ds(my_at, width)] = outb[step, rows_of(me)]

    row_id = lax.broadcasted_iota(jnp.int32, (rows, cols), 0)
    col_id = lax.broadcasted_iota(jnp.int32, (rows, cols), 1)

    def d_range(f):
        ahead = jnp.where(col_id == cols - 1, 0.0, pltpu.roll(f, cols - 1, 1))
        behind = jnp.where(col_id == 0, 0.0, pltpu.roll(f, 1, 1))
        return ahead - behind

    def d_cross(f, before, after):
        ahead = jnp.where(row_id == rows - 1, after, pltpu.roll(f, rows - 1, 0))
        behind = jnp.where(row_id == 0, before, pltpu.roll(f, 1, 0))
        return ahead - behind

    def out_copy(level):
        return pltpu.make_async_copy(chg.at[:, level], out_ref.at[:, level], out_sem.at[level])

    sets = ((pa, ua, va, wa), (pb, ub, vb, wb))
    for k in range(sections):
        step, section = k // 3, k % 3
        po, uo, vo, wo = sets[k % 2]
        pn, un, vn, wn = sets[(k + 1) % 2]
        last = k == sections - 1
        if section == 0:
            spread_all(step).wait_recv()
        if step + 1 < steps:
            spread_some(step + 1, section, 3)
        receive_below(k, po, wo)
        receive_rows(k, 0)
        keep, gain = section_keep[section], section_gain[section]

        def update(i, carry):
            level = jnp.where(i < half, i, jnp.where(i == half, levels - 1, i - 1))

            @pl.when(i == half)
            def _():
                receive_above(k, po, wo)
                receive_rows(k, 1)

            if section == 0:
                frozen = froz[step, 0, level].astype(jnp.float32)
                speed = 1.0 + froz[step, 1, level].astype(jnp.float32)
                advect = half_step * (wind_ref[level] + frozen)
                squared = half_step * (speed * speed)
                adv[level] = advect
                sqr[level] = squared
            else:
                advect = adv[level]
                squared = sqr[level]
            p, u, v, w = po[level + 1], uo[level], vo[level], wo[level + 1]
            p_x, u_x, v_x, w_x = d_range(p), d_range(u), d_range(v), d_range(w)
            p_y = d_cross(p, rrecv[k, 0, pl.ds(2 * level, 1)], rrecv[k, 1, pl.ds(2 * level, 1)])
            v_y = d_cross(
                v, rrecv[k, 0, pl.ds(2 * level + 1, 1)], rrecv[k, 1, pl.ds(2 * level + 1, 1)]
            )
            p_z = po[level + 2] - po[level]
            w_z = wo[level + 2] - wo[level]
            fresh = (
                advect * p_x + squared * (u_x + v_y + w_z),
                advect * u_x + half_step * p_x,
                advect * v_x + half_step * p_y,
                advect * w_x + half_step * p_z,
            )
            new = []
            for field, (rate, old) in enumerate(zip(fresh, (p, u, v, w))):
                change = -rate if section == 0 else keep * chg[field, level] - rate
                if section < 2:
                    chg[field, level] = change
                new.append(old + gain * change)
            if last:
                for field in range(4):
                    chg[field, level] = new[field]
                out_copy(level).start()
            else:
                pn[level + 1], un[level], vn[level], wn[level + 1] = new
                for field, value in ((0, new[0]), (1, new[2])):
                    rsend[k + 1, 0, pl.ds(2 * level + field, 1)] = value[0:1]
                    rsend[k + 1, 1, pl.ds(2 * level + field, 1)] = value[rows - 1 : rows]

                @pl.when(i == 0)
                def _():
                    send_down(k + 1, pn, wn)

                @pl.when(i == half - 1)
                def _():
                    send_rows(k + 1, 0)

                @pl.when(i == half)
                def _():
                    send_up(k + 1, pn, wn)

            return carry

        lax.fori_loop(0, levels, update, 0, unroll=2)
        if not last:
            send_rows(k + 1, 1)

    def stored(level, carry):
        out_copy(level).wait()
        return carry

    lax.fori_loop(0, levels, stored, 0)

    gather_all().wait_send()
    for step in range(steps):
        spread_all(step).wait_send()
    for k in range(sections):
        for side, there in ((0, has_left), (1, has_right)):
            @pl.when(there)
            def _():
                row_copy(k, side, 0).wait_send()
                row_copy(k, side, 1).wait_send()
        for side, there in ((0, has_below), (1, has_above)):
            @pl.when(there)
            def _():
                level_copy(k, side).wait_send()


def body(n, floors, state, turbulence, wind, ground_admittance, ground_kind, drift_cells, drift_eighths):
    fields, levels, rows, cols = state.shape
    steps = drift_cells.shape[0]
    sections = 3 * steps
    width = 2 * levels * cols // n
    f32, bf16 = jnp.float32, jnp.bfloat16
    padded = pltpu.VMEM((levels + 2, rows, cols), f32)
    plain = pltpu.VMEM((levels, rows, cols), f32)
    dma = pltpu.SemaphoreType.DMA
    hbm = pl.BlockSpec(memory_space=pl.ANY)
    return pl.pallas_call(
        functools.partial(kernel, n, floors, steps, levels, rows, cols, width),
        out_shape=jax.ShapeDtypeStruct(state.shape, f32),
        in_specs=[hbm] * 7,
        out_specs=hbm,
        scratch_shapes=[
            pltpu.SMEM((levels,), f32),
            pltpu.VMEM((rows, cols), f32),
            pltpu.VMEM((rows, cols), jnp.int32),
            pltpu.SMEM((steps, levels), jnp.int32),
            pltpu.SMEM((steps, levels), jnp.int32),
            padded, plain, plain, padded,
            padded, plain, plain, padded,
            pltpu.VMEM((fields, levels, rows, cols), f32),
            plain,
            plain,
            pltpu.VMEM((n * rows, width), bf16),
            pltpu.VMEM((steps, n * rows, n * rows), bf16),
            pltpu.VMEM((steps, n * rows, width), bf16),
            pltpu.VMEM((steps, 2, levels, rows, cols), bf16),
            pltpu.VMEM((sections, 2, 2 * levels, cols), f32),
            pltpu.VMEM((sections, 2, 2 * levels, cols), f32),
            pltpu.VMEM((sections, 2, 2, rows, cols), bf16),
            pltpu.VMEM((sections, 2, 2, rows, cols), bf16),
            dma((10,)), dma((levels,)),
            dma, dma,
            dma((steps,)), dma((steps,)),
            dma((sections, 2, 2)), dma((sections, 2, 2)),
            dma((sections, 2)), dma((sections, 2)),
        ],
        compiler_params=pltpu.CompilerParams(
            collective_id=0, has_side_effects=True, vmem_limit_bytes=60 * 2**20
        ),
    )(state, turbulence, wind, ground_admittance, ground_kind, drift_cells, drift_eighths)


def solution(mesh):
    placed = (
        P(None, "height", "cross", None),
        P(None, "height", "cross", None),
        P("height"),
        P("cross", None),
        P("cross", None),
        P(None, "height"),
        P(None, "height"),
    )
    return jax.shard_map(
        functools.partial(body, mesh.shape["cross"], mesh.shape["height"]),
        mesh=mesh,
        in_specs=placed,
        out_specs=P(None, "height", "cross", None),
        check_vma=False,
    )
```
